256 devices in a mesh: blk: 32 (over z, x_hi, core), rel: 8 (over x_lo, y).
Axes of the slice: x: 4 (x_hi: 2, x_lo: 2; x = x_hi * 2 + x_lo), y: 4, z: 8, core: 2. Of those that a mesh axis runs over, the one named last changes fastest.
Arguments:
- left_slab: float32 [524288, 400], P(('blk', 'rel')), may hold values from -1.3 to 1.3
- left_state: float32 [524288], P(('blk', 'rel')), may hold values from 1e-05 to 0.0001
- right_slab: float32 [524288, 400], P(('blk', 'rel')), may hold values from -1.3 to 1.3
- right_state: float32 [524288], P(('blk', 'rel')), may hold values from 1e-05 to 0.0001
- relations: float32 [32, 400], replicated, may hold values from 0.1 to 1.9
- relation_state: float32 [32], replicated, may hold values from 0.01 to 0.2
- src_index: int32 [2, 65536], P(None, ('blk', 'rel')), may hold values from 0 to 2047
- dst_index: int32 [2, 65536], P(None, ('blk', 'rel')), may hold values from 0 to 2047
- relation_id: int32 [2, 65536], P(None, ('blk', 'rel')), may hold values from 0 to 31
- neg_source: int32 [2, 256000], P(None, ('blk', 'rel')), may hold values from 0 to 2047
- neg_target: int32 [2, 256000], P(None, ('blk', 'rel')), may hold values from 0 to 2047
Outputs:
- left_out: float32 [524288, 400], P(('blk', 'rel'))
- right_out: float32 [524288, 400], P(('blk', 'rel'))
- relations_out: float32 [32, 32, 400], P('blk')
The draws below stay inside these ranges and needn't reach their ends.
All inputs are finite; a program needn't handle non-finite values.
Results may differ from the reference program's by a relative error of at most 0.00069.
Values sent between devices are 32-bit elements; how exact they have to be, the bound alone decides.
A program may use at most 64 MiB of HBM per device.

```python
import math
import jax
import jax.numpy as jnp
from jax import lax

D = 400
ROWS = 2048
EDGES = 256
NEG = 1000
NREL = 32
ROUNDS = 2
ENT = 524288
EDGE_ALL = 65536
NEG_ALL = 256000
N_BLK = 32
N_REL = 8


def touch_ends(entries, stream_key, low, top_value):
    index_at = [jax.random.randint(jax.random.fold_in(stream_key, axis), (), 0, length) for axis, length in enumerate(entries.shape)]
    widest = entries.shape.index(max(entries.shape))
    neighbour = index_at[:widest] + [(index_at[widest] + 1) % entries.shape[widest]] + index_at[widest + 1:]
    return entries.at[tuple(index_at)].set(low).at[tuple(neighbour)].set(top_value)


def block_levels(stream_key, extent, cuts, low, top_value):
    def one(position, parts):
        steps = jax.random.uniform(jax.random.fold_in(jax.random.fold_in(stream_key, 6), position), (parts,), jnp.float32, low / len(cuts), top_value / len(cuts))
        return jnp.repeat(jnp.exp(steps), extent[position] // parts).reshape((-1,) + (1,) * (len(extent) - position - 1))

    gain = one(*cuts[0])
    for cut in cuts[1:]:
        gain = gain * one(*cut)
    return gain


def bell_draw(key, shape, deviation, limit, shards=(), held_as=jnp.bfloat16):
    entries = deviation * jax.random.normal(key, shape, jnp.float32)
    if shards:
        entries = entries * block_levels(key, shape, shards, -0.22, 0.18)
    return jnp.clip(entries, -limit, limit).astype(held_as)


def setup_inputs(seed: int = 0) -> dict:
    streams_of = jax.random.split(jax.random.key(seed), 12)
    return {
        "left_slab": bell_draw(streams_of[0], (ENT, D), 0.22, 1.3, ((0, 256),), jnp.float32),
        "left_state": jnp.clip(jnp.exp(math.log(0.0001) - 2.3025851 * jax.random.uniform(streams_of[1], (ENT,), jnp.float32) ** block_levels(streams_of[1], (ENT,), ((0, 256),), -0.2, 0.2)), 9.999999747378752e-06, 0.0001),
        "right_slab": bell_draw(streams_of[2], (ENT, D), 0.22, 1.3, ((0, 256),), jnp.float32),
        "right_state": jnp.clip(jnp.exp(math.log(0.0001) - 2.3025851 * jax.random.uniform(streams_of[3], (ENT,), jnp.float32) ** block_levels(streams_of[3], (ENT,), ((0, 256),), -0.2, 0.2)), 9.999999747378752e-06, 0.0001),
        "relations": jnp.clip(1.0 + 0.18 * jax.random.normal(streams_of[4], (NREL, D), jnp.float32), 0.1, 1.9),
        "relation_state": jnp.clip(jnp.exp(jax.random.uniform(streams_of[5], (NREL,), jnp.float32, math.log(0.01), math.log(0.2))), 0.01, 0.2),
        "src_index": touch_ends(jax.random.randint(streams_of[6], (ROUNDS, EDGE_ALL), 0, ROWS), jax.random.fold_in(streams_of[6], 1), 0, ROWS - 1).astype(jnp.int32),
        "dst_index": touch_ends(jax.random.randint(streams_of[7], (ROUNDS, EDGE_ALL), 0, ROWS), jax.random.fold_in(streams_of[7], 1), 0, ROWS - 1).astype(jnp.int32),
        "relation_id": touch_ends(jax.random.randint(streams_of[8], (ROUNDS, EDGE_ALL), 0, NREL), jax.random.fold_in(streams_of[8], 1), 0, NREL - 1).astype(jnp.int32),
        "neg_source": touch_ends(jax.random.randint(streams_of[9], (ROUNDS, NEG_ALL), 0, ROWS), jax.random.fold_in(streams_of[9], 1), 0, ROWS - 1).astype(jnp.int32),
        "neg_target": touch_ends(jax.random.randint(streams_of[10], (ROUNDS, NEG_ALL), 0, ROWS), jax.random.fold_in(streams_of[10], 1), 0, ROWS - 1).astype(jnp.int32),
    }


rate = 0.1

def adagrad_rows(slab, state, grad):
    new_state = state + lax.optimization_barrier(jnp.mean(grad * grad, axis=1))
    return (slab - rate * grad / jnp.sqrt(new_state)[:, None], new_state)

def train_block(left, lstate, right, rstate, relations, src, dst, rid, nsrc, ndst):
    rows = left.shape[0]
    table = (rid[:, None] == jnp.arange(relations.shape[0], dtype=jnp.int32)[None, :]).astype(jnp.float32)
    weight = jnp.dot(table, relations, precision=lax.Precision.HIGHEST)
    source = left[src]
    target = right[dst]
    pos = lax.optimization_barrier(jnp.sum(source * weight * target, axis=1))
    query = (source * weight).astype(jnp.bfloat16)
    probe = (weight * target).astype(jnp.bfloat16)
    negy = right[ndst].astype(jnp.bfloat16)
    negx = left[nsrc].astype(jnp.bfloat16)
    score_t = jnp.dot(query, negy.T, preferred_element_type=jnp.float32)
    score_s = jnp.dot(probe, negx.T, preferred_element_type=jnp.float32)
    count = score_t.shape[1]
    coef = -jax.nn.sigmoid(-pos)[:, None]
    grad_t = (jax.nn.sigmoid(score_t) / count).astype(jnp.bfloat16)
    grad_s = (jax.nn.sigmoid(score_s) / count).astype(jnp.bfloat16)
    gq = jnp.dot(grad_t, negy, preferred_element_type=jnp.float32)
    gy = jnp.dot(grad_t.T, query, preferred_element_type=jnp.float32)
    gp = jnp.dot(grad_s, negx, preferred_element_type=jnp.float32)
    gx = jnp.dot(grad_s.T, probe, preferred_element_type=jnp.float32)
    g_source = coef * weight * target + gq * weight
    g_target = coef * weight * source + gp * weight
    g_weight = coef * source * target + gq * source + gp * target
    grad_left = jax.ops.segment_sum(g_source, src, num_segments=rows) + jax.ops.segment_sum(gx, nsrc, num_segments=rows)
    grad_right = jax.ops.segment_sum(g_target, dst, num_segments=rows) + jax.ops.segment_sum(gy, ndst, num_segments=rows)
    rel_grad = jnp.dot(table.T, g_weight, precision=lax.Precision.HIGHEST)
    left, lstate = adagrad_rows(left, lstate, grad_left)
    right, rstate = adagrad_rows(right, rstate, grad_right)
    return (left, lstate, right, rstate, rel_grad)

def reference(left_slab, left_state, right_slab, right_state, relations, relation_state, src_index, dst_index, relation_id, neg_source, neg_target):
    blocks = N_BLK * N_REL
    left = left_slab.reshape(blocks, ROWS, D)
    lstate = left_state.reshape(blocks, ROWS)
    right = right_slab.reshape(N_BLK, N_REL, ROWS, D)
    rstate = right_state.reshape(N_BLK, N_REL, ROWS)
    rel_total = jnp.zeros((N_BLK, NREL, D), jnp.float32)
    for step in range(ROUNDS):
        right = jnp.roll(right, 1, axis=0).reshape(blocks, ROWS, D)
        rstate = jnp.roll(rstate, 1, axis=0).reshape(blocks, ROWS)
        src = src_index[step].reshape(blocks, EDGES)
        dst = dst_index[step].reshape(blocks, EDGES)
        rid = relation_id[step].reshape(blocks, EDGES)
        nsrc = neg_source[step].reshape(blocks, NEG)
        ndst = neg_target[step].reshape(blocks, NEG)

        def one(items):
            return train_block(items[0], items[1], items[2], items[3], relations, items[4], items[5], items[6], items[7], items[8])
        left, lstate, right, rstate, rel_grad = lax.map(one, (left, lstate, right, rstate, src, dst, rid, nsrc, ndst))
        rel_total = rel_total + lax.optimization_barrier(jnp.sum(rel_grad.reshape(N_BLK, N_REL, NREL, D), axis=1))
        right = right.reshape(N_BLK, N_REL, ROWS, D)
        rstate = rstate.reshape(N_BLK, N_REL, ROWS)
    new_rstate = relation_state[None, :] + lax.optimization_barrier(jnp.mean(rel_total * rel_total, axis=2))
    relations_out = relations[None] - rate * rel_total / jnp.sqrt(new_rstate)[:, :, None]
    return (left.reshape(ENT, D), right.reshape(ENT, D), relations_out)
```

```python
import jax
import jax.numpy as jnp
from jax import lax
from jax.experimental import pallas as pl
from jax.experimental.pallas import tpu as pltpu
from jax.sharding import PartitionSpec as P

rate = 0.1
D = 400
MAIN = 384
WIDE = 512
LAST = D - MAIN
ROWS = 2048
EDGES = 256
NEG = 1000
NREL = 32
CHUNK = 256
CHUNKS = ROWS // CHUNK
PACKED = CHUNK + ROWS // 128
MESH = pl.DeviceIdType.MESH
f32 = jnp.float32
bf16 = jnp.bfloat16


def iota(shape, axis):
    return lax.broadcasted_iota(jnp.int32, shape, axis)


def dot_nn(a, b):
    return lax.dot_general(a, b, (((1,), (0,)), ((), ())), preferred_element_type=f32)


def dot_nt(a, b):
    return lax.dot_general(a, b, (((1,), (1,)), ((), ())), preferred_element_type=f32)


def dot_tn(a, b):
    return lax.dot_general(a, b, (((0,), (0,)), ((), ())), preferred_element_type=f32)


def halves(x):
    high = x.astype(bf16)
    return high, (x - high.astype(f32)).astype(bf16)


def widen(tail):
    return jnp.concatenate([tail, jnp.zeros((tail.shape[0], 128 - LAST), f32)], axis=1)


def column(table, c):
    lane = iota((128, 128), 1)
    first = jnp.sum(jnp.where(lane == 2 * c, table, 0.0), axis=1, keepdims=True)
    second = jnp.sum(jnp.where(lane == 2 * c + 1, table, 0.0), axis=1, keepdims=True)
    return jnp.concatenate([first, second], axis=0)


def put_column(ref, c, col):
    lane = iota((128, 128), 1)
    old = ref[...]
    new = jnp.where(lane == 2 * c, col[:128], old)
    ref[...] = jnp.where(lane == 2 * c + 1, col[128:], new)


def transposed(rows16):
    return jnp.concatenate([rows16, jnp.zeros((112, 128), f32)], axis=0).T


def eight(ref, rows, columns):
    width = columns.stop - columns.start
    place = iota((8, width), 0)
    out = jnp.broadcast_to(ref[pl.ds(rows[0], 1), columns], (8, width))
    for k in range(1, 8):
        out = jnp.where(place == k, ref[pl.ds(rows[k], 1), columns], out)
    return out


def count_rows(index_row, row_ref, col_ref):
    high = index_row // 128
    low = index_row - 128 * high
    hot_high = jnp.where(iota((16, 1024), 0) == high, 1.0, 0.0).astype(bf16)
    hot_low = jnp.where(iota((128, 1024), 0) == low, 1.0, 0.0).astype(bf16)
    rows = dot_nt(hot_high, hot_low)
    row_ref[...] = rows
    col_ref[...] = transposed(rows)


def negatives(query_ref, slab_ref, row_ref, col_ref, sum_ref, grad_ref):
    sum_ref[...] = jnp.zeros_like(sum_ref)

    def step(c, carry):
        rows = pl.ds(pl.multiple_of(c * CHUNK, CHUNK), CHUNK)
        query = query_ref[...]
        slab = slab_ref[rows, :]
        score = dot_nt(query, slab)
        g = ((0.5 * jnp.tanh(0.5 * score) + 0.5) / NEG).astype(bf16)
        often = jnp.concatenate(
            [row_ref[pl.ds(2 * c, 1), :], row_ref[pl.ds(2 * c + 1, 1), :]], axis=1
        )
        high, low = halves(g.astype(f32) * often)
        sum_ref[...] += dot_nn(high, slab) + dot_nn(low, slab)
        grad_ref[rows, :] = dot_tn(g, query) * column(col_ref[...], c)
        return carry

    lax.fori_loop(0, CHUNKS, step, 0, unroll=2)


def update_chunk(c, rows, index_row, high, low, grad_ref, main_ref, tail_ref, state_ref):
    hot = jnp.where(iota((CHUNK, EDGES), 0) + c * CHUNK == index_row, 1.0, 0.0).astype(bf16)
    grad = grad_ref[rows, :] + dot_nn(hot, high) + dot_nn(hot, low)
    state = column(state_ref[...], c) + jnp.sum(grad * grad, axis=1, keepdims=True) / D
    step = grad * (rate / jnp.sqrt(state))
    return main_ref[rows, 0:MAIN] - step[:, :MAIN], tail_ref[rows, :] - step[:, MAIN:], state


def kernel(
    left,
    lstate,
    right,
    rstate,
    relations,
    relation_state,
    src,
    dst,
    rid,
    src_v,
    dst_v,
    rid_v,
    nsrc_v,
    ndst_v,
    left_out,
    right_out,
    relations_out,
    left_m,
    left_t,
    left_b,
    left_s,
    right_w,
    right_t,
    right_b,
    right_s,
    main0,
    main1,
    pack_in,
    pack0,
    pack1,
    pack_out,
    rel_w,
    drawn,
    often_lr,
    often_lc,
    often_rr,
    often_rc,
    source,
    target,
    weight,
    query,
    probe,
    gq,
    gp,
    grad_l,
    grad_r,
    rel_sum,
    rel_all,
    local_sem,
    send_sem,
    recv_sem,
    rsend_sem,
    rrecv_sem,
):
    blk, rel = lax.axis_index("blk"), lax.axis_index("rel")
    blks, rels = lax.axis_size("blk"), lax.axis_size("rel")
    after = (lax.rem(blk + 1, blks), rel)
    before = (lax.rem(blk + blks - 1, blks), rel)
    core = lax.rem(blk, 2)

    get_right = pltpu.make_async_copy(right, right_w, local_sem.at[0])
    get_left = pltpu.make_async_copy(left, left_m, local_sem.at[1])
    get_right.start()
    get_left.start()

    barrier = pltpu.get_barrier_semaphore()
    pl.semaphore_signal(barrier, inc=1, device_id=before, device_id_type=MESH)
    for k in range(1, rels):
        peer = (blk, lax.rem(rel + k, rels))
        pl.semaphore_signal(barrier, inc=1, device_id=peer, device_id_type=MESH)
    pl.semaphore_wait(barrier, rels)

    def send(src_ref, dst_ref, i):
        return pltpu.make_async_remote_copy(
            src_ref=src_ref,
            dst_ref=dst_ref,
            send_sem=send_sem.at[i],
            recv_sem=recv_sem.at[i],
            device_id=after,
            device_id_type=MESH,
        )

    first_main = send(right.at[:, pl.ds(0, MAIN)], main0, 0)
    first_pack = send(pack_in, pack0, 1)
    first_main.start()

    get_right.wait()
    packed = jnp.zeros((CHUNK, 128), f32)
    for j in range(CHUNKS):
        tail = widen(right_w[j * CHUNK : (j + 1) * CHUNK, MAIN:D])
        packed = packed + (pltpu.roll(tail, LAST * j, 1) if j else tail)
    pack_in[0:CHUNK, :] = packed
    pack_in[CHUNK:PACKED, :] = rstate[...]
    first_pack.start()

    rel_w[:, 0:MAIN] = relations[:, 0:MAIN]
    rel_w[:, MAIN:WIDE] = widen(relations[:, MAIN:D])
    rel_sum[...] = jnp.zeros_like(rel_sum)
    left_s[...] = transposed(lstate[...])
    get_left.wait()
    for j in range(CHUNKS):
        rows = slice(j * CHUNK, (j + 1) * CHUNK)
        tail = widen(left_m[rows, MAIN:D])
        left_t[rows, :] = tail
        left_b[rows, 0:MAIN] = left_m[rows, 0:MAIN].astype(bf16)
        left_b[rows, MAIN:WIDE] = tail.astype(bf16)

    def left_side(t):
        drawn[...] = jnp.full(drawn.shape, -1, jnp.int32)
        drawn[0:1, 0:NEG] = nsrc_v[t : t + 1, :]
        drawn[1:2, 0:NEG] = ndst_v[t : t + 1, :]
        count_rows(drawn[0:1, :], often_lr, often_lc)
        count_rows(drawn[1:2, :], often_rr, often_rc)

        def pick(i, carry):
            at = pl.ds(pl.multiple_of(8 * i, 8), 8)
            rows = [src[t, 8 * i + k] for k in range(8)]
            source[at, 0:MAIN] = eight(left_m, rows, slice(0, MAIN))
            source[at, MAIN:WIDE] = eight(left_t, rows, slice(0, 128))
            rows = [rid[t, 8 * i + k] for k in range(8)]
            weight[at, :] = eight(rel_w, rows, slice(0, WIDE))
            return carry

        lax.fori_loop(0, EDGES // 8, pick, 0, unroll=4)
        query[...] = (source[...] * weight[...]).astype(bf16)

    def right_side(t, main, pack):
        for j in range(CHUNKS):
            rows = slice(j * CHUNK, (j + 1) * CHUNK)
            tail = pack[0:CHUNK, :]
            tail = pltpu.roll(tail, 128 - LAST * j, 1) if j else tail
            tail = jnp.where(iota((CHUNK, 128), 1) < LAST, tail, 0.0)
            right_t[rows, :] = tail
            right_b[rows, 0:MAIN] = main[rows, :].astype(bf16)
            right_b[rows, MAIN:WIDE] = tail.astype(bf16)
        right_s[...] = transposed(pack[CHUNK:PACKED, :])

        def pick(i, carry):
            at = pl.ds(pl.multiple_of(8 * i, 8), 8)
            rows = [dst[t, 8 * i + k] for k in range(8)]
            target[at, 0:MAIN] = eight(main, rows, slice(0, MAIN))
            target[at, MAIN:WIDE] = eight(right_t, rows, slice(0, 128))
            return carry

        lax.fori_loop(0, EDGES // 8, pick, 0, unroll=4)
        probe[...] = (weight[...] * target[...]).astype(bf16)

    def gradients(t):
        negatives(query, right_b, often_rr, often_rc, gq, grad_r)
        negatives(probe, left_b, often_lr, often_lc, gp, grad_l)
        s, w, y = source[...], weight[...], target[...]
        pos = jnp.sum(s * w * y, axis=1, keepdims=True)
        coef = -1.0 / (1.0 + jnp.exp(pos))
        q, p = gq[...], gp[...]
        g_weight = coef * s * y + q * s + p * y
        hot = jnp.where(iota((NREL, EDGES), 0) == rid_v[t : t + 1, :], 1.0, 0.0)
        rel_sum[...] += lax.dot_general(
            hot, g_weight, (((1,), (0,)), ((), ())), precision=lax.Precision.HIGHEST
        )
        return coef * w * y + q * w, coef * w * s + p * w

    left_side(0)
    first_main.wait_recv()
    first_pack.wait_recv()
    right_side(0, main0, pack0)
    g_source, g_target = gradients(0)

    high, low = halves(g_target)
    packed = jnp.zeros((CHUNK, 128), f32)
    second = []
    for c in range(CHUNKS):
        rows = pl.ds(c * CHUNK, CHUNK)
        new_main, new_tail, state = update_chunk(
            c, rows, dst_v[0:1, :], high, low, grad_r, main0, right_t, right_s
        )
        main0[rows, :] = new_main
        packed = packed + (pltpu.roll(new_tail, LAST * c, 1) if c else new_tail)
        put_column(right_s, c, state)
        second.append(send(main0.at[rows, :], main1.at[rows, :], 2 + c))
        second[-1].start()
    pack_out[0:CHUNK, :] = packed
    pack_out[CHUNK:PACKED, :] = right_s[...].T[0:16, :]
    second_pack = send(pack_out, pack1, 2 + CHUNKS)
    second_pack.start()

    high, low = halves(g_source)
    for c in range(CHUNKS):
        rows = pl.ds(c * CHUNK, CHUNK)
        new_main, new_tail, state = update_chunk(
            c, rows, src_v[0:1, :], high, low, grad_l, left_m, left_t, left_s
        )
        left_m[rows, 0:MAIN] = new_main
        left_t[rows, :] = new_tail
        left_b[rows, 0:MAIN] = new_main.astype(bf16)
        left_b[rows, MAIN:WIDE] = new_tail.astype(bf16)
        put_column(left_s, c, state)

    left_side(1)
    second_pack.wait_recv()
    for copy in second:
        copy.wait_recv()
    right_side(1, main1, pack1)
    g_source, g_target = gradients(1)

    rel_all[rel] = rel_sum[...]
    shares = []
    for k in range(1, rels):
        shares.append(
            pltpu.make_async_remote_copy(
                src_ref=rel_sum,
                dst_ref=rel_all.at[rel],
                send_sem=rsend_sem.at[k],
                recv_sem=rrecv_sem.at[k],
                device_id=(blk, lax.rem(rel + k, rels)),
                device_id_type=MESH,
            )
        )
        shares[-1].start()

    puts = []
    high, low = halves(g_target)
    for c in range(CHUNKS):
        rows = pl.ds(c * CHUNK, CHUNK)
        new_main, new_tail, _ = update_chunk(
            c, rows, dst_v[1:2, :], high, low, grad_r, main1, right_t, right_s
        )
        right_w[rows, 0:MAIN] = new_main
        right_w[rows, MAIN:D] = new_tail[:, :LAST]
        puts.append(pltpu.make_async_copy(right_w.at[rows, :], right_out.at[rows, :], local_sem.at[2 + c]))
        puts[-1].start()
    high, low = halves(g_source)
    for c in range(CHUNKS):
        rows = pl.ds(c * CHUNK, CHUNK)
        new_main, new_tail, _ = update_chunk(
            c, rows, src_v[1:2, :], high, low, grad_l, left_m, left_t, left_s
        )
        left_m[rows, 0:MAIN] = new_main
        left_m[rows, MAIN:D] = new_tail[:, :LAST]
        puts.append(
            pltpu.make_async_copy(
                left_m.at[rows, :], left_out.at[rows, :], local_sem.at[2 + CHUNKS + c]
            )
        )
        puts[-1].start()

    for share in shares:
        share.wait_recv()
    total = rel_all[0]
    for k in range(1, rels):
        total = total + rel_all[k]
    own = jnp.broadcast_to(relation_state[...], (NREL, NREL))
    own = jnp.sum(jnp.where(iota((NREL, NREL), 0) == iota((NREL, NREL), 1), own, 0.0), axis=1, keepdims=True)
    state = own + jnp.sum(total * total, axis=1, keepdims=True) / D
    new = rel_w[...] - rate * total / jnp.sqrt(state)
    relations_out[0, :, :] = new[:, :D]

    first_main.wait_send()
    first_pack.wait_send()
    for copy in second:
        copy.wait_send()
    second_pack.wait_send()
    for share in shares:
        share.wait_send()
    for put in puts:
        put.wait()


def local(
    left_slab,
    left_state,
    right_slab,
    right_state,
    relations,
    relation_state,
    src_index,
    dst_index,
    relation_id,
    neg_source,
    neg_target,
):
    vmem = pl.BlockSpec(memory_space=pltpu.VMEM)
    smem = pl.BlockSpec(memory_space=pltpu.SMEM)
    hbm = pl.BlockSpec(memory_space=pltpu.HBM)
    rels = lax.axis_size("rel")
    edge = pltpu.VMEM((EDGES, WIDE), f32)
    return pl.pallas_call(
        kernel,
        out_shape=(
            jax.ShapeDtypeStruct((ROWS, D), f32),
            jax.ShapeDtypeStruct((ROWS, D), f32),
            jax.ShapeDtypeStruct((1, NREL, D), f32),
        ),
        in_specs=[hbm, vmem, hbm, vmem, vmem, vmem, smem, smem, smem, vmem, vmem, vmem, vmem, vmem],
        out_specs=(hbm, hbm, vmem),
        scratch_shapes=[
            pltpu.VMEM((ROWS, D), f32),
            pltpu.VMEM((ROWS, 128), f32),
            pltpu.VMEM((ROWS, WIDE), bf16),
            pltpu.VMEM((128, 128), f32),
            pltpu.VMEM((ROWS, D), f32),
            pltpu.VMEM((ROWS, 128), f32),
            pltpu.VMEM((ROWS, WIDE), bf16),
            pltpu.VMEM((128, 128), f32),
            pltpu.VMEM((ROWS, MAIN), f32),
            pltpu.VMEM((ROWS, MAIN), f32),
            pltpu.VMEM((PACKED, 128), f32),
            pltpu.VMEM((PACKED, 128), f32),
            pltpu.VMEM((PACKED, 128), f32),
            pltpu.VMEM((PACKED, 128), f32),
            pltpu.VMEM((NREL, WIDE), f32),
            pltpu.VMEM((8, 1024), jnp.int32),
            pltpu.VMEM((16, 128), f32),
            pltpu.VMEM((128, 128), f32),
            pltpu.VMEM((16, 128), f32),
            pltpu.VMEM((128, 128), f32),
            edge,
            edge,
            edge,
            pltpu.VMEM((EDGES, WIDE), bf16),
            pltpu.VMEM((EDGES, WIDE), bf16),
            edge,
            edge,
            pltpu.VMEM((ROWS, WIDE), f32),
            pltpu.VMEM((ROWS, WIDE), f32),
            pltpu.VMEM((NREL, WIDE), f32),
            pltpu.VMEM((rels, NREL, WIDE), f32),
            pltpu.SemaphoreType.DMA((2 + 2 * CHUNKS,)),
            pltpu.SemaphoreType.DMA((3 + CHUNKS,)),
            pltpu.SemaphoreType.DMA((3 + CHUNKS,)),
            pltpu.SemaphoreType.DMA((rels,)),
            pltpu.SemaphoreType.DMA((rels,)),
        ],
        compiler_params=pltpu.CompilerParams(
            collective_id=0, has_side_effects=True, vmem_limit_bytes=56 * 2**20
        ),
        name="train",
    )(
        left_slab,
        left_state.reshape(ROWS // 128, 128),
        right_slab,
        right_state.reshape(ROWS // 128, 128),
        relations,
        relation_state.reshape(1, NREL),
        src_index,
        dst_index,
        relation_id,
        src_index,
        dst_index,
        relation_id,
        neg_source,
        neg_target,
    )


def solution(mesh):
    in_specs = (
        P(("blk", "rel"), None),
        P(("blk", "rel")),
        P(("blk", "rel"), None),
        P(("blk", "rel")),
        P(),
        P(),
        P(None, ("blk", "rel")),
        P(None, ("blk", "rel")),
        P(None, ("blk", "rel")),
        P(None, ("blk", "rel")),
        P(None, ("blk", "rel")),
    )
    out_specs = (P(("blk", "rel"), None), P(("blk", "rel"), None), P("blk", None, None))
    return jax.shard_map(local, mesh=mesh, in_specs=in_specs, out_specs=out_specs, check_vma=False)
```

```python
import jax
import jax.numpy as jnp
from jax import lax
from jax.experimental import pallas as pl
from jax.experimental.pallas import tpu as pltpu
from jax.sharding import PartitionSpec as P

rate = 0.1
D = 400
ROWS = 2048
EDGES = 256
NEG = 1000
NREL = 32
CHUNK = 256
CHUNKS = ROWS // CHUNK
PIECES = 5
FLIGHT = 3
LATER = {2: 5, 7: 6}
MESH = pl.DeviceIdType.MESH
f32 = jnp.float32
bf16 = jnp.bfloat16


def iota(shape, axis):
    return lax.broadcasted_iota(jnp.int32, shape, axis)


def dot(a, b, ca, cb, precision=None):
    return lax.dot_general(
        a, b, (((ca,), (cb,)), ((), ())), precision=precision, preferred_element_type=f32
    )


def halves(x):
    high = x.astype(bf16)
    return high, (x - high.astype(f32)).astype(bf16)


def cut(c):
    return slice(c * CHUNK, (c + 1) * CHUNK)


def hot_chunk(index_row, c):
    return jnp.where(iota((CHUNK, EDGES), 0) + c * CHUNK == index_row, 1.0, 0.0).astype(bf16)


def count_rows(index_row):
    high = index_row // 128
    low = index_row - 128 * high
    hot_high = jnp.where(iota((16, 1024), 0) == high, 1.0, 0.0).astype(bf16)
    hot_low = jnp.where(iota((128, 1024), 0) == low, 1.0, 0.0).astype(bf16)
    return dot(hot_high, hot_low, 1, 1)


def kernel(
    left,
    lstate,
    right,
    rstate,
    relations,
    relation_state,
    src,
    dst,
    rid,
    nsrc,
    ndst,
    left_m,
    main1,
    rel_all,
    rel_old,
    rel_state,
    left_b,
    left_s,
    right_b,
    main0,
    state0,
    state1,
    drawn,
    often_l,
    often_r,
    hot_src,
    hot_dst,
    source,
    target,
    weight,
    query,
    query_t,
    probe,
    probe_t,
    gq,
    gp,
    grad_l,
    grad_r,
    rel_sum,
    local_sem,
    send_sem,
    recv_sem,
    rsend_sem,
    rrecv_sem,
):

    blk, rel = lax.axis_index("blk"), lax.axis_index("rel")
    blks, rels = lax.axis_size("blk"), lax.axis_size("rel")
    after = (lax.rem(blk + 1, blks), rel)
    before = (lax.rem(blk + blks - 1, blks), rel)
    core = lax.rem(blk, 2)

    get_left = pltpu.make_async_copy(left, left_m, local_sem.at[0])
    get_left.start()

    barrier = pltpu.get_barrier_semaphore()
    pl.semaphore_signal(barrier, inc=1, device_id=before, device_id_type=MESH)
    for k in range(1, rels):
        peer = (blk, lax.rem(rel + k, rels))
        pl.semaphore_signal(barrier, inc=1, device_id=peer, device_id_type=MESH)
    pl.semaphore_wait(barrier, rels)

    def send(src_ref, dst_ref, t, i):
        return pltpu.make_async_remote_copy(
            src_ref=src_ref,
            dst_ref=dst_ref,
            send_sem=send_sem.at[t, i],
            recv_sem=recv_sem.at[t, i],
            device_id=after,
            device_id_type=MESH,
        )

    mains, states = (main0, main1), (state0, state1)
    moves = (
        [send(right.at[:, cut(c)], main0.at[:, cut(c)], 0, c) for c in range(CHUNKS)]
        + [send(rstate, state0, 0, CHUNKS)],
        [send(main0.at[:, cut(c)], main1.at[:, cut(c)], 1, c) for c in range(CHUNKS)]
        + [send(state0, state1, 1, CHUNKS)],
    )
    for move in moves[0]:
        move.start()

    rel_old[...] = relations[...]
    own = jnp.broadcast_to(relation_state[...], (NREL, NREL))
    diagonal = iota((NREL, NREL), 0) == iota((NREL, NREL), 1)
    own = jnp.sum(jnp.where(diagonal, own, 0.0), axis=1, keepdims=True)
    rel_state[...] = jnp.broadcast_to(own, (NREL, 128))
    left_s[...] = lstate[...]
    get_left.wait()

    def left_side(t):
        drawn[...] = jnp.full(drawn.shape, -1, jnp.int32)
        drawn[0:1, 0:NEG] = nsrc[t : t + 1, :]
        drawn[1:2, 0:NEG] = ndst[t : t + 1, :]
        often_l[...] = count_rows(drawn[0:1, :])
        often_r[...] = count_rows(drawn[1:2, :])
        hot_rel = jnp.where(iota((NREL, EDGES), 0) == rid[t : t + 1, :], 1.0, 0.0)
        weight[...] = dot(relations[...], hot_rel, 0, 0, lax.Precision.HIGHEST)
        source[...] = jnp.zeros_like(source)
        for c in range(CHUNKS):
            hot_src[cut(c), :] = hot_chunk(src[t : t + 1, :], c)
            hot_dst[cut(c), :] = hot_chunk(dst[t : t + 1, :], c)
            pick(left_m, left_b, hot_src, source, c)
        q = source[...] * weight[...]
        query_t[...] = q.astype(bf16)
        query[...] = q.T.astype(bf16)

    def pick(main, rounded, hot, out, c):
        x = main[:, cut(c)]
        high = x.astype(bf16)
        rest = x - high.astype(f32)
        middle, low = halves(rest)
        rounded[:, cut(c)] = high
        table = hot[cut(c), :]
        out[...] += dot(high, table, 1, 0) + (dot(middle, table, 1, 0) + dot(low, table, 1, 0))

    def negatives(mine, mine_t, slab, often, sum_ref, grad_ref, c):
        rows = slab[:, cut(c)]
        score = dot(mine[...], rows, 1, 0)
        g = ((0.5 * jnp.tanh(0.5 * score) + 0.5) / NEG).astype(bf16)
        times = jnp.concatenate([often[2 * c : 2 * c + 1, :], often[2 * c + 1 : 2 * c + 2, :]], axis=1)
        sum_ref[...] += dot(rows, (g.astype(f32) * times).astype(bf16), 1, 1)
        grad_ref[:, cut(c)] = dot(mine_t[...], g, 1, 0) * times

    def feed(c):
        @pl.when(core == 1)
        def _():
            moves[1][c - FLIGHT].wait_send()
            moves[1][c].start()

    def gradients(t):
        target[...] = jnp.zeros_like(target)
        gq[...] = jnp.zeros_like(gq)
        gp[...] = jnp.zeros_like(gp)
        moves[t][CHUNKS].wait_recv()
        for c in range(CHUNKS):
            moves[t][c].wait_recv()
            pick(mains[t], right_b, hot_dst, target, c)
            negatives(query, query_t, right_b, often_r, gq, grad_r, c)
            if t == 1 and c in LATER:
                feed(LATER[c])
        p = weight[...] * target[...]
        probe_t[...] = p.astype(bf16)
        probe[...] = p.T.astype(bf16)
        for c in range(CHUNKS):
            negatives(probe, probe_t, left_b, often_l, gp, grad_l, c)
        if t == 1:
            feed(7)
        s, w, y = source[...], weight[...], target[...]
        pos = jnp.sum(s * w * y, axis=0, keepdims=True)
        coef = -1.0 / (1.0 + jnp.exp(pos))
        q, p = gq[...], gp[...]
        g_weight = coef * s * y + q * s + p * y
        hot_rel = jnp.where(iota((NREL, EDGES), 0) == rid[t : t + 1, :], 1.0, 0.0)
        g_rel = dot(hot_rel, g_weight, 1, 1, lax.Precision.HIGHEST)
        return coef * w * y + q * w, coef * w * s + p * w, g_rel

    def update(c, high, low, hot, grad_ref, main, state):
        table = hot[cut(c), :]
        grad = grad_ref[:, cut(c)] + (dot(high, table, 1, 1) + dot(low, table, 1, 1))
        new_state = state[:, cut(c)] + jnp.sum(grad * grad, axis=0, keepdims=True) / D
        state[:, cut(c)] = new_state
        main[:, cut(c)] = main[:, cut(c)] - grad * (rate / jnp.sqrt(new_state))

    left_side(0)
    g_source, g_target, g_rel = gradients(0)
    rel_sum[...] = g_rel
    high, low = halves(g_target)
    for c in range(CHUNKS):
        update(c, high, low, hot_dst, grad_r, main0, state0)
        if c < FLIGHT:
            moves[1][c].start()
        else:

            @pl.when(core == 0)
            def _():
                moves[1][c].start()

    moves[1][CHUNKS].start()
    high, low = halves(g_source)
    for c in range(CHUNKS):
        update(c, high, low, hot_src, grad_l, left_m, left_s)

    left_side(1)
    feed(3)
    feed(4)
    g_source, g_target, g_rel = gradients(1)
    rel_sum[...] += g_rel
    rel_all[rel] = rel_sum[...]
    shares = []
    for k in range(1, rels):
        shares.append(
            pltpu.make_async_remote_copy(
                src_ref=rel_sum,
                dst_ref=rel_all.at[rel],
                send_sem=rsend_sem.at[k],
                recv_sem=rrecv_sem.at[k],
                device_id=(blk, lax.rem(rel + k, rels)),
                device_id_type=MESH,
            )
        )
        shares[-1].start()

    high, low = halves(g_target)
    for c in range(CHUNKS):
        update(c, high, low, hot_dst, grad_r, main1, state1)

    high, low = halves(g_source)
    for c in range(CHUNKS):
        update(c, high, low, hot_src, grad_l, left_m, left_s)

    for move in moves[0] + moves[1][CHUNKS - FLIGHT :]:
        move.wait_send()

    @pl.when(core == 0)
    def _():
        for move in moves[1][: CHUNKS - FLIGHT]:
            move.wait_send()

    for copy in shares:
        copy.wait()


def put_out(
    left, right, rel_all, rel_old, rel_state, left_out, right_out, relations_out, sem
):
    puts = []
    for c in range(PIECES):
        rows = slice(c * (D // PIECES), (c + 1) * (D // PIECES))
        puts.append(pltpu.make_async_copy(left.at[rows, :], left_out.at[rows, :], sem.at[2 * c]))
        puts.append(pltpu.make_async_copy(right.at[rows, :], right_out.at[rows, :], sem.at[2 * c + 1]))
    for put in puts:
        put.start()
    total = rel_all[0]
    for k in range(1, rel_all.shape[0]):
        total = total + rel_all[k]
    state = rel_state[:, 0:1] + jnp.sum(total * total, axis=1, keepdims=True) / D
    relations_out[0, :, :] = rel_old[...] - rate * total / jnp.sqrt(state)
    for put in puts:
        put.wait()


def local(
    left_slab,
    left_state,
    right_slab,
    right_state,
    relations,
    relation_state,
    src_index,
    dst_index,
    relation_id,
    neg_source,
    neg_target,
):
    vmem = pl.BlockSpec(memory_space=pltpu.VMEM)
    hbm = pl.BlockSpec(memory_space=pltpu.HBM)
    rels = lax.axis_size("rel")
    slab = pltpu.VMEM((D, ROWS), f32)
    rounded = pltpu.VMEM((D, ROWS), bf16)
    row = pltpu.VMEM((1, ROWS), f32)
    hot = pltpu.VMEM((ROWS, EDGES), bf16)
    edge = pltpu.VMEM((D, EDGES), f32)
    pin = pltpu.with_memory_space_constraint
    given = (
        left_slab.T,
        left_state.reshape(1, ROWS),
        right_slab.T,
        right_state.reshape(1, ROWS),
        relations,
        relation_state.reshape(1, NREL),
        src_index,
        dst_index,
        relation_id,
        neg_source,
        neg_target,
    )
    held = pl.pallas_call(
        kernel,
        out_shape=(
            pltpu.VMEM((D, ROWS), f32),
            pltpu.VMEM((D, ROWS), f32),
            pltpu.VMEM((rels, NREL, D), f32),
            pltpu.VMEM((NREL, D), f32),
            pltpu.VMEM((NREL, 128), f32),
        ),
        in_specs=[hbm, vmem, hbm] + [vmem] * 8,
        out_specs=(vmem,) * 5,
        scratch_shapes=[
            rounded,
            row,
            rounded,
            slab,
            row,
            row,
            pltpu.VMEM((8, 1024), jnp.int32),
            pltpu.VMEM((16, 128), f32),
            pltpu.VMEM((16, 128), f32),
            hot,
            hot,
            edge,
            edge,
            edge,
            pltpu.VMEM((EDGES, D), bf16),
            pltpu.VMEM((D, EDGES), bf16),
            pltpu.VMEM((EDGES, D), bf16),
            pltpu.VMEM((D, EDGES), bf16),
            edge,
            edge,
            slab,
            slab,
            pltpu.VMEM((NREL, D), f32),
            pltpu.SemaphoreType.DMA((1,)),
            pltpu.SemaphoreType.DMA((2, CHUNKS + 1)),
            pltpu.SemaphoreType.DMA((2, CHUNKS + 1)),
            pltpu.SemaphoreType.DMA((rels,)),
            pltpu.SemaphoreType.DMA((rels,)),
        ],
        compiler_params=pltpu.CompilerParams(
            collective_id=0, has_side_effects=True, vmem_limit_bytes=40 * 2**20
        ),
        name="train",
    )(*[pin(x, pltpu.HBM) for x in given])
    left, right, relations_out = pl.pallas_call(
        put_out,
        out_shape=(
            jax.ShapeDtypeStruct((D, ROWS), f32),
            jax.ShapeDtypeStruct((D, ROWS), f32),
            jax.ShapeDtypeStruct((1, NREL, D), f32),
        ),
        in_specs=[vmem, vmem, vmem, vmem, vmem],
        out_specs=(hbm, hbm, vmem),
        scratch_shapes=[pltpu.SemaphoreType.DMA((2 * PIECES,))],
        compiler_params=pltpu.CompilerParams(vmem_limit_bytes=4 * 2**20),
        name="put_out",
    )(*[pin(x, pltpu.VMEM) for x in held])
    return left.T, right.T, relations_out


def solution(mesh):
    in_specs = (
        P(("blk", "rel"), None),
        P(("blk", "rel")),
        P(("blk", "rel"), None),
        P(("blk", "rel")),
        P(),
        P(),
        P(None, ("blk", "rel")),
        P(None, ("blk", "rel")),
        P(None, ("blk", "rel")),
        P(None, ("blk", "rel")),
        P(None, ("blk", "rel")),
    )
    out_specs = (P(("blk", "rel"), None), P(("blk", "rel"), None), P("blk", None, None))
    return jax.shard_map(local, mesh=mesh, in_specs=in_specs, out_specs=out_specs, check_vma=False)
```

```python
import jax
import jax.numpy as jnp
from jax import lax
from jax.experimental import pallas as pl
from jax.experimental.pallas import tpu as pltpu
from jax.sharding import PartitionSpec as P

rate = 0.1
D = 400
ROWS = 2048
EDGES = 256
NEG = 1000
NREL = 32
CHUNK = 256
CHUNKS = ROWS // CHUNK
PIECES = 2
FLIGHT = 3
LATER = {2: 6, 7: 7}
MESH = pl.DeviceIdType.MESH
f32 = jnp.float32
bf16 = jnp.bfloat16


def iota(shape, axis):
    return lax.broadcasted_iota(jnp.int32, shape, axis)


def dot(a, b, ca, cb, precision=None):
    return lax.dot_general(
        a, b, (((ca,), (cb,)), ((), ())), precision=precision, preferred_element_type=f32
    )


def halves(x):
    high = x.astype(bf16)
    return high, (x - high.astype(f32)).astype(bf16)


def cut(c):
    return slice(c * CHUNK, (c + 1) * CHUNK)


def hot_chunk(index_row, c):
    return jnp.where(iota((CHUNK, EDGES), 0) + c * CHUNK == index_row, 1.0, 0.0).astype(bf16)


def count_rows(index_row):
    high = index_row // 128
    low = index_row - 128 * high
    hot_high = jnp.where(iota((16, 1024), 0) == high, 1.0, 0.0).astype(bf16)
    hot_low = jnp.where(iota((128, 1024), 0) == low, 1.0, 0.0).astype(bf16)
    return dot(hot_high, hot_low, 1, 1)


def kernel(
    left,
    lstate,
    right,
    rstate,
    relations,
    relation_state,
    src_in,
    dst_in,
    rid_in,
    nsrc_in,
    ndst_in,
    left_m,
    main1,
    rel_all,
    rel_old,
    rel_state,
    rel_row,
    src,
    dst,
    rid,
    nsrc,
    ndst,
    left_b,
    left_s,
    right_b,
    main0,
    state0,
    state1,
    drawn,
    often_l,
    often_r,
    hot_src,
    hot_dst,
    source,
    target,
    weight,
    query,
    query_t,
    probe,
    probe_t,
    gq,
    gp,
    g_left,
    grad_r,
    rel_sum,
    rel_pair,
    local_sem,
    send_sem,
    recv_sem,
    rsend_sem,
    rrecv_sem,
):

    blk, rel = lax.axis_index("blk"), lax.axis_index("rel")
    blks, rels = lax.axis_size("blk"), lax.axis_size("rel")
    after = (lax.rem(blk + 1, blks), rel)
    before = (lax.rem(blk + blks - 1, blks), rel)
    core = lax.rem(blk, 2)

    barrier = pltpu.get_barrier_semaphore()
    pl.semaphore_signal(barrier, inc=1, device_id=before, device_id_type=MESH)
    for k in range(1, rels):
        peer = (blk, lax.rem(rel + k, rels))
        pl.semaphore_signal(barrier, inc=1, device_id=peer, device_id_type=MESH)
    pairs = (
        (src_in, src),
        (dst_in, dst),
        (rid_in, rid),
        (nsrc_in, nsrc),
        (ndst_in, ndst),
        (relations, rel_old),
        (relation_state, rel_row),
        (lstate, left_s),
        (left, left_m),
    )
    gets = [pltpu.make_async_copy(a, b, local_sem.at[i]) for i, (a, b) in enumerate(pairs)]
    for get in gets:
        get.start()
    pl.semaphore_wait(barrier, rels)

    def send(src_ref, dst_ref, t, i):
        return pltpu.make_async_remote_copy(
            src_ref=src_ref,
            dst_ref=dst_ref,
            send_sem=send_sem.at[t, i],
            recv_sem=recv_sem.at[t, i],
            device_id=after,
            device_id_type=MESH,
        )

    mains, states = (main0, main1), (state0, state1)
    moves = (
        [send(right.at[:, cut(c)], main0.at[:, cut(c)], 0, c) for c in range(CHUNKS)]
        + [send(rstate, state0, 0, CHUNKS)],
        [send(main0.at[:, cut(c)], main1.at[:, cut(c)], 1, c) for c in range(CHUNKS)]
        + [send(state0, state1, 1, CHUNKS)],
    )
    for move in moves[0]:
        move.start()

    for get in gets:
        get.wait()
    own = jnp.broadcast_to(rel_row[...], (NREL, NREL))
    diagonal = iota((NREL, NREL), 0) == iota((NREL, NREL), 1)
    own = jnp.sum(jnp.where(diagonal, own, 0.0), axis=1, keepdims=True)
    rel_state[...] = jnp.broadcast_to(own, (NREL, 128))

    def left_side(t):
        drawn[...] = jnp.full(drawn.shape, -1, jnp.int32)
        drawn[0:1, 0:NEG] = nsrc[t : t + 1, :]
        drawn[1:2, 0:NEG] = ndst[t : t + 1, :]
        often_l[...] = count_rows(drawn[0:1, :])
        often_r[...] = count_rows(drawn[1:2, :])
        hot_rel = jnp.where(iota((NREL, EDGES), 0) == rid[t : t + 1, :], 1.0, 0.0)
        weight[...] = dot(rel_old[...], hot_rel, 0, 0, lax.Precision.HIGHEST)
        source[...] = jnp.zeros_like(source)
        for c in range(CHUNKS):
            hot_src[cut(c), :] = hot_chunk(src[t : t + 1, :], c)
            hot_dst[cut(c), :] = hot_chunk(dst[t : t + 1, :], c)
            pick(left_m, left_b, hot_src, source, c)
        q = source[...] * weight[...]
        query_t[...] = q.astype(bf16)
        query[...] = q.T.astype(bf16) * 0.5

    def pick(main, rounded, hot, out, c):
        x = main[:, cut(c)]
        high = x.astype(bf16)
        rest = x - high.astype(f32)
        middle, low = halves(rest)
        rounded[:, cut(c)] = high
        table = hot[cut(c), :]
        out[...] += dot(high, table, 1, 0) + (dot(middle, table, 1, 0) + dot(low, table, 1, 0))

    def times(often, c):
        return jnp.concatenate([often[2 * c : 2 * c + 1, :], often[2 * c + 1 : 2 * c + 2, :]], axis=1)

    def slope(mine, rows):
        half_score = dot(mine[...], rows, 1, 0)
        return (jnp.tanh(half_score) * (0.5 / NEG) + 0.5 / NEG).astype(bf16)

    def feed(c):
        @pl.when(core == 1)
        def _():
            moves[1][c - FLIGHT].wait_send()
            moves[1][c].start()

    def gradients(t, share):
        target[...] = jnp.zeros_like(target)
        gq[...] = jnp.zeros_like(gq)
        gp[...] = jnp.zeros_like(gp)
        moves[t][CHUNKS].wait_recv()
        for c in range(CHUNKS):
            moves[t][c].wait_recv()
            pick(mains[t], right_b, hot_dst, target, c)
            rows = right_b[:, cut(c)]
            g = slope(query, rows)
            gq[...] += dot(rows, (g.astype(f32) * times(often_r, c)).astype(bf16), 1, 1)
            grad_r[:, cut(c)] = dot(query_t[...], g, 1, 0) * times(often_r, c)
            if t == 1 and c in LATER:
                feed(LATER[c])
        p = weight[...] * target[...]
        probe_t[...] = p.astype(bf16)
        probe[...] = p.T.astype(bf16) * 0.5
        for c in range(0, CHUNKS, 2):
            both = slice(c * CHUNK, (c + 2) * CHUNK)
            rows = left_b[:, both]
            g = slope(probe, rows)
            g_left[:, both] = g
            often = jnp.concatenate([times(often_l, c), times(often_l, c + 1)], axis=1)
            gp[...] += dot(rows, (g.astype(f32) * often).astype(bf16), 1, 1)
        s, w, y = source[...], weight[...], target[...]
        pos = jnp.sum(s * w * y, axis=0, keepdims=True)
        coef = -1.0 / (1.0 + jnp.exp(pos))
        q, p = gq[...], gp[...]
        g_weight = coef * s * y + q * s + p * y
        hot_rel = jnp.where(iota((NREL, EDGES), 0) == rid[t : t + 1, :], 1.0, 0.0).astype(bf16)
        high, low = halves(g_weight)
        share(dot(hot_rel, high, 1, 1) + dot(hot_rel, low, 1, 1))
        return coef * w * y + q * w, coef * w * s + p * w

    def update(c, high, low, hot, drawn_grad, main, state):
        table = hot[cut(c), :]
        grad = drawn_grad + (dot(high, table, 1, 1) + dot(low, table, 1, 1))
        new_state = state[:, cut(c)] + jnp.sum(grad * grad, axis=0, keepdims=True) / D
        state[:, cut(c)] = new_state
        main[:, cut(c)] = main[:, cut(c)] - grad * (rate / jnp.sqrt(new_state))

    def left_grad(c):
        return dot(probe_t[...], g_left[:, cut(c)], 1, 0) * times(often_l, c)

    def keep(g_rel):
        rel_sum[...] = g_rel

    left_side(0)
    g_source, g_target = gradients(0, keep)
    high, low = halves(g_target)
    for c in range(CHUNKS):
        update(c, high, low, hot_dst, grad_r[:, cut(c)], main0, state0)
        if c < FLIGHT:
            moves[1][c].start()
        else:

            @pl.when(core == 0)
            def _():
                moves[1][c].start()

    moves[1][CHUNKS].start()
    high, low = halves(g_source)
    for c in range(CHUNKS):
        update(c, high, low, hot_src, left_grad(c), left_m, left_s)

    left_side(1)
    feed(3)
    feed(4)
    feed(5)
    def share_with(peer, src_ref, dst_ref, k):
        return pltpu.make_async_remote_copy(
            src_ref=src_ref,
            dst_ref=dst_ref,
            send_sem=rsend_sem.at[k],
            recv_sem=rrecv_sem.at[k],
            device_id=(blk, peer),
            device_id_type=MESH,
        )

    half = rels // 2
    place = lax.rem(rel, half)
    to_all = [
        share_with(lax.rem(rel + k, rels), rel_sum, rel_all.at[rel], k) for k in range(1, rels)
    ]
    to_pair = share_with(lax.rem(rel + half, rels), rel_sum, rel_pair, 0)
    to_side = [
        share_with(
            rel - place + lax.rem(place + k, half), rel_all.at[place], rel_all.at[place], k
        )
        for k in range(1, half)
    ]

    def exchange(g_rel):
        rel_sum[...] += g_rel

        @pl.when(core == 0)
        def _():
            for copy in to_all:
                copy.start()
            rel_all[rel] = rel_sum[...]

        @pl.when(core == 1)
        def _():
            to_pair.start()
            for k in range(half, rels):
                rel_all[k] = jnp.zeros((NREL, D), f32)

    g_source, g_target = gradients(1, exchange)
    high, low = halves(g_target)
    for c in range(CHUNKS):
        update(c, high, low, hot_dst, grad_r[:, cut(c)], main1, state1)

    @pl.when(core == 1)
    def _():
        to_pair.wait_recv()
        rel_all[place] = rel_sum[...] + rel_pair[...]
        for copy in to_side:
            copy.start()


    high, low = halves(g_source)
    for c in range(CHUNKS):
        update(c, high, low, hot_src, left_grad(c), left_m, left_s)

    for move in moves[0] + moves[1][CHUNKS - FLIGHT :]:
        move.wait_send()

    @pl.when(core == 0)
    def _():
        for move in moves[1][: CHUNKS - FLIGHT]:
            move.wait_send()

    @pl.when(core == 0)
    def _():
        for copy in to_all:
            copy.wait()

    @pl.when(core == 1)
    def _():
        to_pair.wait_send()
        for copy in to_side:
            copy.wait()


def put_out(
    left, right, rel_all, rel_old, rel_state, left_out, right_out, relations_out, rel_new, sem
):
    puts = []
    for c in range(PIECES):
        rows = slice(c * (D // PIECES), (c + 1) * (D // PIECES))
        puts.append(pltpu.make_async_copy(left.at[rows, :], left_out.at[rows, :], sem.at[2 * c]))
        puts.append(pltpu.make_async_copy(right.at[rows, :], right_out.at[rows, :], sem.at[2 * c + 1]))
    for put in puts:
        put.start()
    total = rel_all[0]
    for k in range(1, rel_all.shape[0]):
        total = total + rel_all[k]
    state = rel_state[:, 0:1] + jnp.sum(total * total, axis=1, keepdims=True) / D
    rel_new[0, :, :] = rel_old[...] - rate * total / jnp.sqrt(state)
    puts.append(pltpu.make_async_copy(rel_new, relations_out, sem.at[2 * PIECES]))
    puts[-1].start()
    for put in puts:
        put.wait()


def local(
    left_slab,
    left_state,
    right_slab,
    right_state,
    relations,
    relation_state,
    src_index,
    dst_index,
    relation_id,
    neg_source,
    neg_target,
):
    vmem = pl.BlockSpec(memory_space=pltpu.VMEM)
    hbm = pl.BlockSpec(memory_space=pltpu.HBM)
    rels = lax.axis_size("rel")
    slab = pltpu.VMEM((D, ROWS), f32)
    rounded = pltpu.VMEM((D, ROWS), bf16)
    row = pltpu.VMEM((1, ROWS), f32)
    hot = pltpu.VMEM((ROWS, EDGES), bf16)
    edge = pltpu.VMEM((D, EDGES), f32)
    pin = pltpu.with_memory_space_constraint
    given = (
        left_slab.T,
        left_state.reshape(1, ROWS),
        right_slab.T,
        right_state.reshape(1, ROWS),
        relations,
        relation_state.reshape(1, NREL),
        src_index,
        dst_index,
        relation_id,
        neg_source,
        neg_target,
    )
    held = pl.pallas_call(
        kernel,
        out_shape=(
            pltpu.VMEM((D, ROWS), f32),
            pltpu.VMEM((D, ROWS), f32),
            pltpu.VMEM((rels, NREL, D), f32),
            pltpu.VMEM((NREL, D), f32),
            pltpu.VMEM((NREL, 128), f32),
        ),
        in_specs=[hbm] * 11,
        out_specs=(vmem,) * 5,
        scratch_shapes=[
            pltpu.VMEM((1, NREL), f32),
            pltpu.VMEM((2, EDGES), jnp.int32),
            pltpu.VMEM((2, EDGES), jnp.int32),
            pltpu.VMEM((2, EDGES), jnp.int32),
            pltpu.VMEM((2, NEG), jnp.int32),
            pltpu.VMEM((2, NEG), jnp.int32),
            rounded,
            row,
            rounded,
            slab,
            row,
            row,
            pltpu.VMEM((8, 1024), jnp.int32),
            pltpu.VMEM((16, 128), f32),
            pltpu.VMEM((16, 128), f32),
            hot,
            hot,
            edge,
            edge,
            edge,
            pltpu.VMEM((EDGES, D), bf16),
            pltpu.VMEM((D, EDGES), bf16),
            pltpu.VMEM((EDGES, D), bf16),
            pltpu.VMEM((D, EDGES), bf16),
            edge,
            edge,
            pltpu.VMEM((EDGES, ROWS), bf16),
            slab,
            pltpu.VMEM((NREL, D), f32),
            pltpu.VMEM((NREL, D), f32),
            pltpu.SemaphoreType.DMA((9,)),
            pltpu.SemaphoreType.DMA((2, CHUNKS + 1)),
            pltpu.SemaphoreType.DMA((2, CHUNKS + 1)),
            pltpu.SemaphoreType.DMA((rels,)),
            pltpu.SemaphoreType.DMA((rels,)),
        ],
        compiler_params=pltpu.CompilerParams(
            collective_id=0, has_side_effects=True, vmem_limit_bytes=40 * 2**20
        ),
        name="train",
    )(*[pin(x, pltpu.HBM) for x in given])
    left, right, relations_out = pl.pallas_call(
        put_out,
        out_shape=(
            jax.ShapeDtypeStruct((D, ROWS), f32),
            jax.ShapeDtypeStruct((D, ROWS), f32),
            jax.ShapeDtypeStruct((1, NREL, D), f32),
        ),
        in_specs=[vmem, vmem, vmem, vmem, vmem],
        out_specs=(hbm, hbm, hbm),
        scratch_shapes=[
            pltpu.VMEM((1, NREL, D), f32),
            pltpu.SemaphoreType.DMA((2 * PIECES + 1,)),
        ],
        compiler_params=pltpu.CompilerParams(vmem_limit_bytes=4 * 2**20),
        name="put_out",
    )(*[pin(x, pltpu.VMEM) for x in held])
    return left.T, right.T, relations_out


def solution(mesh):
    in_specs = (
        P(("blk", "rel"), None),
        P(("blk", "rel")),
        P(("blk", "rel"), None),
        P(("blk", "rel")),
        P(),
        P(),
        P(None, ("blk", "rel")),
        P(None, ("blk", "rel")),
        P(None, ("blk", "rel")),
        P(None, ("blk", "rel")),
        P(None, ("blk", "rel")),
    )
    out_specs = (P(("blk", "rel"), None), P(("blk", "rel"), None), P("blk", None, None))
    return jax.shard_map(local, mesh=mesh, in_specs=in_specs, out_specs=out_specs, check_vma=False)
```

```python
import jax
import jax.numpy as jnp
from jax import lax
from jax.experimental import pallas as pl
from jax.experimental.pallas import tpu as pltpu
from jax.sharding import PartitionSpec as P

rate = 0.1
D = 400
ROWS = 2048
EDGES = 256
NEG = 1000
NREL = 32
CHUNK = 256
SPANS = [(k, k + CHUNK) for k in range(0, ROWS - CHUNK, CHUNK)]
SPANS += [(ROWS - CHUNK, ROWS - CHUNK // 2), (ROWS - CHUNK // 2, ROWS)]
CHUNKS = len(SPANS)
PIECES = 2
FLIGHT = 3
LATER = {2: 6, 5: 7, 7: 8}
MESH = pl.DeviceIdType.MESH
f32 = jnp.float32
bf16 = jnp.bfloat16


def iota(shape, axis):
    return lax.broadcasted_iota(jnp.int32, shape, axis)


def dot(a, b, ca, cb, precision=None):
    return lax.dot_general(
        a, b, (((ca,), (cb,)), ((), ())), precision=precision, preferred_element_type=f32
    )


def halves(x):
    high = x.astype(bf16)
    return high, (x - high.astype(f32)).astype(bf16)


def cut(c):
    return slice(*SPANS[c])


def hot_chunk(index_row, c):
    start, stop = SPANS[c]
    return jnp.where(iota((stop - start, EDGES), 0) + start == index_row, 1.0, 0.0).astype(bf16)


def count_rows(index_row):
    high = index_row // 128
    low = index_row - 128 * high
    hot_high = jnp.where(iota((16, 1024), 0) == high, 1.0, 0.0).astype(bf16)
    hot_low = jnp.where(iota((128, 1024), 0) == low, 1.0, 0.0).astype(bf16)
    return dot(hot_high, hot_low, 1, 1)


def kernel(
    left,
    lstate,
    right,
    rstate,
    relations,
    relation_state,
    src_in,
    dst_in,
    rid_in,
    nsrc_in,
    ndst_in,
    left_m,
    main1,
    rel_all,
    rel_old,
    rel_state,
    rel_row,
    src,
    dst,
    rid,
    nsrc,
    ndst,
    left_b,
    left_s,
    right_b,
    main0,
    state0,
    state1,
    drawn,
    often_l,
    often_r,
    hot_src,
    hot_dst,
    source,
    target,
    weight,
    query,
    query_t,
    probe,
    probe_t,
    gq,
    gp,
    g_left,
    grad_r,
    rel_sum,
    rel_pair,
    local_sem,
    send_sem,
    recv_sem,
    rsend_sem,
    rrecv_sem,
):

    blk, rel = lax.axis_index("blk"), lax.axis_index("rel")
    blks, rels = lax.axis_size("blk"), lax.axis_size("rel")
    after = (lax.rem(blk + 1, blks), rel)
    before = (lax.rem(blk + blks - 1, blks), rel)
    core = lax.rem(blk, 2)

    barrier = pltpu.get_barrier_semaphore()
    pl.semaphore_signal(barrier, inc=1, device_id=before, device_id_type=MESH)
    for k in range(1, rels):
        peer = (blk, lax.rem(rel + k, rels))
        pl.semaphore_signal(barrier, inc=1, device_id=peer, device_id_type=MESH)
    pl.semaphore_wait(barrier, rels)

    def send(src_ref, dst_ref, t, i):
        return pltpu.make_async_remote_copy(
            src_ref=src_ref,
            dst_ref=dst_ref,
            send_sem=send_sem.at[t, i],
            recv_sem=recv_sem.at[t, i],
            device_id=after,
            device_id_type=MESH,
        )

    mains, states = (main0, main1), (state0, state1)
    moves = (
        [send(right.at[:, cut(c)], main0.at[:, cut(c)], 0, c) for c in range(CHUNKS)]
        + [send(rstate, state0, 0, CHUNKS)],
        [send(main0.at[:, cut(c)], main1.at[:, cut(c)], 1, c) for c in range(CHUNKS)]
        + [send(state0, state1, 1, CHUNKS)],
    )
    for move in moves[0]:
        move.start()
    pairs = (
        (src_in, src),
        (dst_in, dst),
        (rid_in, rid),
        (nsrc_in, nsrc),
        (ndst_in, ndst),
        (relations, rel_old),
        (relation_state, rel_row),
        (lstate, left_s),
        (left, left_m),
    )
    gets = [pltpu.make_async_copy(a, b, local_sem.at[i]) for i, (a, b) in enumerate(pairs)]
    for get in gets:
        get.start()

    for get in gets:
        get.wait()
    own = jnp.broadcast_to(rel_row[...], (NREL, NREL))
    diagonal = iota((NREL, NREL), 0) == iota((NREL, NREL), 1)
    own = jnp.sum(jnp.where(diagonal, own, 0.0), axis=1, keepdims=True)
    rel_state[...] = jnp.broadcast_to(own, (NREL, 128))

    def left_side(t):
        drawn[...] = jnp.full(drawn.shape, -1, jnp.int32)
        drawn[0:1, 0:NEG] = nsrc[t : t + 1, :]
        drawn[1:2, 0:NEG] = ndst[t : t + 1, :]
        often_l[...] = count_rows(drawn[0:1, :])
        often_r[...] = count_rows(drawn[1:2, :])
        hot_rel = jnp.where(iota((NREL, EDGES), 0) == rid[t : t + 1, :], 1.0, 0.0)
        weight[...] = dot(rel_old[...], hot_rel, 0, 0, lax.Precision.HIGHEST)
        source[...] = jnp.zeros_like(source)
        for c in range(CHUNKS):
            hot_src[cut(c), :] = hot_chunk(src[t : t + 1, :], c)
            hot_dst[cut(c), :] = hot_chunk(dst[t : t + 1, :], c)
            pick(left_m, left_b, hot_src, source, c)
        q = source[...] * weight[...]
        query_t[...] = q.astype(bf16)
        query[...] = q.T.astype(bf16) * 0.5

    def pick(main, rounded, hot, out, c):
        x = main[:, cut(c)]
        high = x.astype(bf16)
        rest = x - high.astype(f32)
        middle, low = halves(rest)
        rounded[:, cut(c)] = high
        table = hot[cut(c), :]
        out[...] += dot(high, table, 1, 0) + (dot(middle, table, 1, 0) + dot(low, table, 1, 0))

    def times(often, c):
        return times_of(often, *SPANS[c])

    def times_of(often, start, stop):
        pieces = [often[k : k + 1, :] for k in range(start // 128, stop // 128)]
        return pieces[0] if len(pieces) == 1 else jnp.concatenate(pieces, axis=1)

    def slope(mine, rows):
        half_score = dot(mine[...], rows, 1, 0)
        return (jnp.tanh(half_score) * (0.5 / NEG) + 0.5 / NEG).astype(bf16)

    def feed(c):
        @pl.when(core == 1)
        def _():
            moves[1][c - FLIGHT].wait_send()
            moves[1][c].start()

    def gradients(t, share):
        target[...] = jnp.zeros_like(target)
        gq[...] = jnp.zeros_like(gq)
        gp[...] = jnp.zeros_like(gp)
        moves[t][CHUNKS].wait_recv()
        for c in range(CHUNKS):
            moves[t][c].wait_recv()
            pick(mains[t], right_b, hot_dst, target, c)
            rows = right_b[:, cut(c)]
            g = slope(query, rows)
            gq[...] += dot(rows, (g.astype(f32) * times(often_r, c)).astype(bf16), 1, 1)
            grad_r[:, cut(c)] = dot(query_t[...], g, 1, 0) * times(often_r, c)
            if t == 1 and c in LATER:
                feed(LATER[c])
        p = weight[...] * target[...]
        probe_t[...] = p.astype(bf16)
        probe[...] = p.T.astype(bf16) * 0.5
        for start in range(0, ROWS, 2 * CHUNK):
            both = slice(start, start + 2 * CHUNK)
            rows = left_b[:, both]
            g = slope(probe, rows)
            g_left[:, both] = g
            often = times_of(often_l, start, start + 2 * CHUNK)
            gp[...] += dot(rows, (g.astype(f32) * often).astype(bf16), 1, 1)
        s, w, y = source[...], weight[...], target[...]
        pos = jnp.sum(s * w * y, axis=0, keepdims=True)
        coef = -1.0 / (1.0 + jnp.exp(pos))
        q, p = gq[...], gp[...]
        g_weight = coef * s * y + q * s + p * y
        hot_rel = jnp.where(iota((NREL, EDGES), 0) == rid[t : t + 1, :], 1.0, 0.0).astype(bf16)
        high, low = halves(g_weight)
        share(dot(hot_rel, high, 1, 1) + dot(hot_rel, low, 1, 1))
        return coef * w * y + q * w, coef * w * s + p * w

    def update(c, high, low, hot, drawn_grad, main, state):
        table = hot[cut(c), :]
        grad = drawn_grad + (dot(high, table, 1, 1) + dot(low, table, 1, 1))
        new_state = state[:, cut(c)] + jnp.sum(grad * grad, axis=0, keepdims=True) / D
        state[:, cut(c)] = new_state
        main[:, cut(c)] = main[:, cut(c)] - grad * (rate / jnp.sqrt(new_state))

    def left_grad(c):
        return dot(probe_t[...], g_left[:, cut(c)], 1, 0) * times(often_l, c)

    def keep(g_rel):
        rel_sum[...] = g_rel

    left_side(0)
    g_source, g_target = gradients(0, keep)
    high, low = halves(g_target)
    for c in range(CHUNKS):
        update(c, high, low, hot_dst, grad_r[:, cut(c)], main0, state0)
        if c < FLIGHT:
            moves[1][c].start()
        else:

            @pl.when(core == 0)
            def _():
                moves[1][c].start()

    moves[1][CHUNKS].start()
    high, low = halves(g_source)
    for c in range(CHUNKS):
        update(c, high, low, hot_src, left_grad(c), left_m, left_s)

    left_side(1)
    feed(3)
    feed(4)
    feed(5)
    def share_with(peer, src_ref, dst_ref, k):
        return pltpu.make_async_remote_copy(
            src_ref=src_ref,
            dst_ref=dst_ref,
            send_sem=rsend_sem.at[k],
            recv_sem=rrecv_sem.at[k],
            device_id=(blk, peer),
            device_id_type=MESH,
        )

    half = rels // 2
    place = lax.rem(rel, half)
    side = lax.div(rel, half)
    to_all = [
        share_with(
            half * lax.rem(side + dx, 2) + lax.rem(place + dy, half),
            rel_sum,
            rel_all.at[rel],
            half * dx + dy,
        )
        for dx in (1, 0)
        for dy in (2, 1, 3, 0)
        if dx or dy
    ]
    to_pair = share_with(lax.rem(rel + half, rels), rel_sum, rel_pair, 0)
    to_side = [
        share_with(
            rel - place + lax.rem(place + k, half), rel_all.at[place], rel_all.at[place], k
        )
        for k in range(1, half)
    ]

    def exchange(g_rel):
        rel_sum[...] += g_rel

        @pl.when(core == 0)
        def _():
            for copy in to_all:
                copy.start()
            rel_all[rel] = rel_sum[...]

        @pl.when(core == 1)
        def _():
            for k in range(half, rels):
                rel_all[k] = jnp.zeros((NREL, D), f32)

    g_source, g_target = gradients(1, exchange)
    high, low = halves(g_target)
    for c in range(CHUNKS):
        update(c, high, low, hot_dst, grad_r[:, cut(c)], main1, state1)
    high, low = halves(g_source)
    for c in range(CHUNKS):
        update(c, high, low, hot_src, left_grad(c), left_m, left_s)

    for move in moves[0] + moves[1][CHUNKS - FLIGHT :]:
        move.wait_send()

    @pl.when(core == 0)
    def _():
        for move in moves[1][: CHUNKS - FLIGHT]:
            move.wait_send()

    @pl.when(core == 0)
    def _():
        for copy in to_all:
            copy.wait()

    @pl.when(core == 1)
    def _():
        to_pair.start()
        to_pair.wait_recv()
        rel_all[place] = rel_sum[...] + rel_pair[...]
        for copy in to_side:
            copy.start()
        to_pair.wait_send()
        for copy in to_side:
            copy.wait()


def put_out(
    left, right, rel_all, rel_old, rel_state, left_out, right_out, relations_out, rel_new, sem
):
    puts = []
    for c in range(PIECES):
        rows = slice(c * (D // PIECES), (c + 1) * (D // PIECES))
        puts.append(pltpu.make_async_copy(left.at[rows, :], left_out.at[rows, :], sem.at[2 * c]))
        puts.append(pltpu.make_async_copy(right.at[rows, :], right_out.at[rows, :], sem.at[2 * c + 1]))
    for put in puts:
        put.start()
    total = rel_all[0]
    for k in range(1, rel_all.shape[0]):
        total = total + rel_all[k]
    state = rel_state[:, 0:1] + jnp.sum(total * total, axis=1, keepdims=True) / D
    rel_new[0, :, :] = rel_old[...] - rate * total / jnp.sqrt(state)
    puts.append(pltpu.make_async_copy(rel_new, relations_out, sem.at[2 * PIECES]))
    puts[-1].start()
    for put in puts:
        put.wait()


def local(
    left_slab,
    left_state,
    right_slab,
    right_state,
    relations,
    relation_state,
    src_index,
    dst_index,
    relation_id,
    neg_source,
    neg_target,
):
    vmem = pl.BlockSpec(memory_space=pltpu.VMEM)
    hbm = pl.BlockSpec(memory_space=pltpu.HBM)
    rels = lax.axis_size("rel")
    slab = pltpu.VMEM((D, ROWS), f32)
    rounded = pltpu.VMEM((D, ROWS), bf16)
    row = pltpu.VMEM((1, ROWS), f32)
    hot = pltpu.VMEM((ROWS, EDGES), bf16)
    edge = pltpu.VMEM((D, EDGES), f32)
    pin = pltpu.with_memory_space_constraint
    given = (
        left_slab.T,
        left_state.reshape(1, ROWS),
        right_slab.T,
        right_state.reshape(1, ROWS),
        relations,
        relation_state.reshape(1, NREL),
        src_index,
        dst_index,
        relation_id,
        neg_source,
        neg_target,
    )
    held = pl.pallas_call(
        kernel,
        out_shape=(
            pltpu.VMEM((D, ROWS), f32),
            pltpu.VMEM((D, ROWS), f32),
            pltpu.VMEM((rels, NREL, D), f32),
            pltpu.VMEM((NREL, D), f32),
            pltpu.VMEM((NREL, 128), f32),
        ),
        in_specs=[hbm] * 11,
        out_specs=(vmem,) * 5,
        scratch_shapes=[
            pltpu.VMEM((1, NREL), f32),
            pltpu.VMEM((2, EDGES), jnp.int32),
            pltpu.VMEM((2, EDGES), jnp.int32),
            pltpu.VMEM((2, EDGES), jnp.int32),
            pltpu.VMEM((2, NEG), jnp.int32),
            pltpu.VMEM((2, NEG), jnp.int32),
            rounded,
            row,
            rounded,
            slab,
            row,
            row,
            pltpu.VMEM((8, 1024), jnp.int32),
            pltpu.VMEM((16, 128), f32),
            pltpu.VMEM((16, 128), f32),
            hot,
            hot,
            edge,
            edge,
            edge,
            pltpu.VMEM((EDGES, D), bf16),
            pltpu.VMEM((D, EDGES), bf16),
            pltpu.VMEM((EDGES, D), bf16),
            pltpu.VMEM((D, EDGES), bf16),
            edge,
            edge,
            pltpu.VMEM((EDGES, ROWS), bf16),
            slab,
            pltpu.VMEM((NREL, D), f32),
            pltpu.VMEM((NREL, D), f32),
            pltpu.SemaphoreType.DMA((9,)),
            pltpu.SemaphoreType.DMA((2, CHUNKS + 1)),
            pltpu.SemaphoreType.DMA((2, CHUNKS + 1)),
            pltpu.SemaphoreType.DMA((rels,)),
            pltpu.SemaphoreType.DMA((rels,)),
        ],
        compiler_params=pltpu.CompilerParams(
            collective_id=0, has_side_effects=True, vmem_limit_bytes=40 * 2**20
        ),
        name="train",
    )(*[pin(x, pltpu.HBM) for x in given])
    left, right, relations_out = pl.pallas_call(
        put_out,
        out_shape=(
            jax.ShapeDtypeStruct((D, ROWS), f32),
            jax.ShapeDtypeStruct((D, ROWS), f32),
            jax.ShapeDtypeStruct((1, NREL, D), f32),
        ),
        in_specs=[vmem, vmem, vmem, vmem, vmem],
        out_specs=(hbm, hbm, hbm),
        scratch_shapes=[
            pltpu.VMEM((1, NREL, D), f32),
            pltpu.SemaphoreType.DMA((2 * PIECES + 1,)),
        ],
        compiler_params=pltpu.CompilerParams(vmem_limit_bytes=4 * 2**20),
        name="put_out",
    )(*[pin(x, pltpu.VMEM) for x in held])
    return left.T, right.T, relations_out


def solution(mesh):
    in_specs = (
        P(("blk", "rel"), None),
        P(("blk", "rel")),
        P(("blk", "rel"), None),
        P(("blk", "rel")),
        P(),
        P(),
        P(None, ("blk", "rel")),
        P(None, ("blk", "rel")),
        P(None, ("blk", "rel")),
        P(None, ("blk", "rel")),
        P(None, ("blk", "rel")),
    )
    out_specs = (P(("blk", "rel"), None), P(("blk", "rel"), None), P("blk", None, None))
    return jax.shard_map(local, mesh=mesh, in_specs=in_specs, out_specs=out_specs, check_vma=False)
```
